512 devices in a mesh: fsdp: 128 (over y, z, core), rep: 4 (over x).
Axes of the slice: x: 4, y: 4, z: 16, core: 2. Of those that a mesh axis runs over, the one named last changes fastest.
Arguments:
- partials: bfloat16 [4, 8192, 8192], P('rep', 'fsdp'), may hold values from -20 to 20
- factor_stats: float32 [128, 4, 512, 512], P('fsdp', 'rep'), may hold values from -64 to 34816, as said below
- owner_slots: int32 [256], replicated, may hold values from 0 to 255, each once
Outputs:
- update: bfloat16 [8192, 8192], P(('fsdp', 'rep'))
The draws below stay inside these ranges and needn't reach their ends.
Inputs may be any that keep to these rules, and one draw needn't show every extreme that they name: `owner_slots`: every pair slot owns exactly one block. Each matrix factor_stats[o, r] is symmetric with a positive diagonal that exceeds the sum of the magnitudes of the other entries of its row.
All inputs are finite; a program needn't handle non-finite values.
Results may differ from the reference program's by a relative error of at most 0.015.
Values may be sent and summed in bfloat16 or wider, within the bound.
No kernel may reach another device: no remote copies, remote signals or barrier semaphores. Data moves between devices by JAX's collectives and lax.ppermute only.
A program may use at most 64 MiB of HBM per device.

```python
import jax
import jax.numpy as jnp
from jax import lax

D = 8192
B = 512
ITERS = 2
POWER_STEPS = 6
ROWS = 8192
NB = 256
N_FSDP = 128
N_REP = 4


def draw_partials(key, part):
    key = jax.random.fold_in(key, 11)
    subkeys = jax.random.split(key, 4)
    row_scale = jnp.exp(jax.random.uniform(subkeys[0], (1, ROWS, 1), jnp.float32, -1.15, 1.15))
    column_scale = jnp.exp(jax.random.uniform(subkeys[1], (1, 1, D), jnp.float32, -1.15, 1.15))
    values = 0.5 * jnp.clip(jax.random.normal(subkeys[3], (N_REP, ROWS, D), jnp.float32), -4.0, 4.0)
    return (values * row_scale * column_scale).astype(jnp.bfloat16)


def draw_factor_stats(key, part):
    key = jax.random.fold_in(key, 23)
    subkeys = jax.random.split(key, 3)
    top_log = 2.3
    matrix_count = N_FSDP * N_REP
    scales = jnp.exp(jax.random.uniform(subkeys[0], (matrix_count, B), jnp.float32, 0.0, top_log))
    magnitude = jax.random.uniform(subkeys[1], (matrix_count, B, B), jnp.float32, 0.5, 1.0)
    sign_pattern = jax.random.rademacher(subkeys[2], (matrix_count, B, B), dtype=jnp.float32)
    entries = magnitude * sign_pattern
    upper = jnp.arange(B)[:, None] < jnp.arange(B)[None, :]
    symmetric = jnp.where(upper[None], entries, jnp.swapaxes(entries, 1, 2))
    identity = jnp.eye(B, dtype=jnp.float32)
    off_diagonal = symmetric * scales[:, :, None] * scales[:, None, :] * (1.0 - identity)
    diagonal = 1.05 * B * jnp.exp(top_log) * scales
    stats = 0.25 * (off_diagonal + identity[None] * diagonal[:, :, None])
    return stats.reshape(N_FSDP, N_REP, B, B).astype(jnp.float32)


def setup_inputs(seed: int = 0) -> dict:
    keys = jax.random.split(jax.random.key(seed), 4)
    return {
        "partials": draw_partials(jax.random.fold_in(keys[3], 71), 0),
        "factor_stats": draw_factor_stats(jax.random.fold_in(keys[3], 71), 0),
        "owner_slots": jax.random.permutation(keys[2], NB).astype(jnp.int32),
    }


HIGHEST = lax.Precision.HIGHEST
EPSILON = 1e-06

def inverse_fourth_root(statistic):
    order_size = statistic.shape[0]
    identity = jnp.eye(order_size, dtype=jnp.float32)
    vector = jnp.ones((order_size,), jnp.float32)
    for power_step in range(POWER_STEPS):
        image = jnp.dot(statistic, vector, precision=HIGHEST)
        vector = image * lax.rsqrt(jnp.sum(image * image) + EPSILON)
    largest = jnp.sum(vector * jnp.dot(statistic, vector, precision=HIGHEST))
    matrix = statistic / largest
    inverse_root = identity
    for newton_step in range(ITERS):
        factor = (5.0 * identity - matrix) * 0.25
        inverse_root = jnp.dot(inverse_root, factor, precision=HIGHEST)
        if newton_step + 1 < ITERS:
            square = jnp.dot(factor, factor, precision=HIGHEST)
            fourth = jnp.dot(square, square, precision=HIGHEST)
            matrix = jnp.dot(fourth, matrix, precision=HIGHEST)
    return inverse_root

def reference(partials, factor_stats, owner_slots):
    summed = partials[0].astype(jnp.float32)
    for replica in range(1, N_REP):
        summed = summed + partials[replica].astype(jnp.float32)
    summed = summed.astype(jnp.bfloat16)
    band_count = ROWS // B
    column_count = D // B
    blocks = summed.reshape(band_count, B, column_count, B).transpose(0, 2, 1, 3).reshape(NB, B, B)
    slot_stats = factor_stats.reshape(NB, 2, B, B)

    def one_block(operands):
        gradient, slot_index = operands
        both_stats = lax.dynamic_index_in_dim(slot_stats, slot_index, 0, keepdims=False)
        left_stat = both_stats[0] + jnp.dot(gradient, gradient.T, preferred_element_type=jnp.float32)
        right_stat = both_stats[1] + jnp.dot(gradient.T, gradient, preferred_element_type=jnp.float32)
        left_root = inverse_fourth_root(left_stat)
        right_root = inverse_fourth_root(right_stat)
        gradient_wide = gradient.astype(jnp.float32)
        raw_update = jnp.dot(jnp.dot(left_root, gradient_wide, precision=HIGHEST), right_root, precision=HIGHEST)
        graft_scale = jnp.sqrt(jnp.sum(gradient_wide * gradient_wide) + EPSILON) * lax.rsqrt(jnp.sum(raw_update * raw_update) + EPSILON)
        return (raw_update * graft_scale).astype(jnp.bfloat16)
    updates = lax.map(one_block, (blocks, owner_slots))
    return updates.reshape(band_count, column_count, B, B).transpose(0, 2, 1, 3).reshape(ROWS, D)
```

```python
import jax
import jax.numpy as jnp
from jax import lax
from jax.experimental import pallas as pl
from jax.experimental.pallas import tpu as pltpu
from jax.sharding import Mesh
from jax.sharding import PartitionSpec as P

POWER_STEPS = 6
EPSILON = 1e-06

PLANE = ("y", "zq", "zl", "core")
EVERYONE = PLANE + ("rep",)

BF16 = jnp.bfloat16
F32 = jnp.float32


def matmul(a, b, contract=((1,), (0,))):
    return lax.dot_general(a, b, (contract, ((), ())), preferred_element_type=F32)


def grid_of(shape):
    return (
        lax.broadcasted_iota(jnp.int32, shape, 0),
        lax.broadcasted_iota(jnp.int32, shape, 1),
    )


def pack_statistic(stat):
    half = stat.shape[0] // 2
    first, cross, last = stat[:half, :half], stat[:half, half:], stat[half:, half:]
    row, col = grid_of((half, half))
    folded = jnp.where(row <= col, first, last)
    diagonal = jnp.sum(jnp.where(row == col, last, 0.0), axis=0)
    packed = jnp.concatenate([folded, cross], axis=1).astype(BF16)
    return packed, diagonal.astype(BF16)


def select_kernel(source_ref, table_ref, out_ref):
    count = out_ref.shape[0]

    def body(index, carry):
        out_ref[index] = table_ref[source_ref[index]]
        return carry

    lax.fori_loop(0, count, body, 0, unroll=16)


def select_rows(source, table):
    return pl.pallas_call(
        select_kernel,
        out_shape=jax.ShapeDtypeStruct(table.shape, table.dtype),
        in_specs=[
            pl.BlockSpec(memory_space=pltpu.SMEM),
            pl.BlockSpec(memory_space=pltpu.VMEM),
        ],
        out_specs=pl.BlockSpec(memory_space=pltpu.VMEM),
        name="select_rows",
    )(source, table)


def unfold(packed_ref, diagonal, stat_ref):
    half = packed_ref.shape[0]
    folded = packed_ref[:, :half].astype(F32)
    cross = packed_ref[:, half:].astype(F32)
    row, col = grid_of((half, half))
    turned = folded.T
    stat_ref[:half, :half] += jnp.where(row <= col, folded, turned)
    lower = jnp.where(row > col, folded, turned)
    stat_ref[half:, half:] += jnp.where(row == col, diagonal, lower)
    stat_ref[:half, half:] += cross
    stat_ref[half:, :half] += cross.T


def main_kernel(
    place_ref, packed_ref, diagonals_ref, pieces_ref, out_ref, grad_ref, left_ref, right_ref
):
    core, zl = place_ref[0], place_ref[1]
    cores, steps, rows, size = pieces_ref.shape
    for step in range(steps):
        origin = lax.rem(zl - step + steps, steps)
        for member in range(cores):
            first = pl.multiple_of((origin * cores + member) * rows, rows)
            grad_ref[pl.ds(first, rows), :] = pieces_ref[member, step]
    gradient = grad_ref[...]
    left_ref[...] = matmul(gradient, gradient, ((1,), (1,)))
    right_ref[...] = matmul(gradient.T, gradient)
    unfold(packed_ref.at[0], diagonals_ref[0:1, :].astype(F32), left_ref)
    unfold(packed_ref.at[1], diagonals_ref[1:2, :].astype(F32), right_ref)
    roots = []
    row, col = grid_of((size, size))
    identity = jnp.where(row == col, 1.0, 0.0)
    images = [jnp.sum(ref[...], axis=0, keepdims=True) for ref in (left_ref, right_ref)]
    for power_step in range(POWER_STEPS):
        vectors = [image * lax.rsqrt(jnp.sum(image * image) + EPSILON) for image in images]
        axis = 1 - power_step % 2
        images = [
            jnp.sum(ref[...] * vector, axis=axis, keepdims=True)
            for ref, vector in zip((left_ref, right_ref), vectors)
        ]
    for ref, vector, image in zip((left_ref, right_ref), vectors, images):
        turned = jnp.sum(identity * vector, axis=0, keepdims=True)
        largest = jnp.sum(turned * image)
        scaled = ref[...] * (1.0 / largest)
        narrow = scaled.astype(BF16)
        second = matmul(narrow, narrow)
        square = (25.0 / 16.0) * identity - (10.0 / 16.0) * scaled + (1.0 / 16.0) * second
        times = (1.25 * scaled - 0.25 * second).astype(BF16)
        narrow = square.astype(BF16)
        fourth = matmul(narrow, narrow).astype(BF16)
        last = matmul(fourth, times)
        roots.append((25.0 / 16.0) * identity - (5.0 / 16.0) * scaled - 0.25 * last)
    left, right = roots
    half_way = matmul(left.astype(BF16), gradient)
    raw = matmul(half_way.astype(BF16), right.astype(BF16))
    wide = gradient.astype(F32)
    scale = jnp.sqrt(jnp.sum(wide * wide) + EPSILON) * lax.rsqrt(
        jnp.sum(raw * raw) + EPSILON
    )
    left_ref[...] = raw * scale
    for origin in range(steps):
        first = pl.multiple_of(origin * cores * rows + core * rows, rows)
        out_ref[origin] = left_ref[pl.ds(first, rows), :].astype(BF16)


def precondition(place, packed, diagonals, pieces):
    size = pieces.shape[-1]
    vmem = pl.BlockSpec(memory_space=pltpu.VMEM)
    return pl.pallas_call(
        main_kernel,
        out_shape=jax.ShapeDtypeStruct(pieces.shape[1:], BF16),
        in_specs=[pl.BlockSpec(memory_space=pltpu.SMEM), vmem, vmem, vmem],
        out_specs=vmem,
        scratch_shapes=[
            pltpu.VMEM((size, size), BF16),
            pltpu.VMEM((size, size), F32),
            pltpu.VMEM((size, size), F32),
        ],
        compiler_params=pltpu.CompilerParams(vmem_limit_bytes=40 * 2**20),
        name="precondition",
    )(place, packed, diagonals, pieces)


def on_device(partials, factor_stats, owner_slots):
    rows, width = partials.shape[1:]
    size = factor_stats.shape[-1]
    reps, zls, cores = (lax.axis_size(name) for name in ("rep", "zl", "core"))
    everyone = lax.axis_size(EVERYONE)
    me = lax.axis_index(EVERYONE)
    core, zl, rep = (lax.axis_index(name) for name in ("core", "zl", "rep"))

    source = 2 * owner_slots.reshape(-1, 1, reps) + jnp.arange(2, dtype=jnp.int32)[None, :, None]
    source = source.reshape(everyone)

    parts = partials[0].reshape(rows, zls, reps, size).transpose(2, 1, 0, 3)
    summed = lax.psum_scatter(parts, "rep", scatter_dimension=0, tiled=False)

    packed, diagonal = pack_statistic(factor_stats[0, 0])
    both = source.reshape(-1, 2, reps)
    both = jnp.broadcast_to(both.transpose(0, 2, 1)[:, None], (both.shape[0], cores, reps, 2))
    mine = both.reshape(everyone, 2) == me
    diagonals = lax.psum_scatter(
        jnp.where(mine[:, :, None], diagonal, jnp.zeros((), BF16)),
        EVERYONE,
        scatter_dimension=0,
        tiled=False,
    )
    tiles = packed.reshape(size // 16, 4, 2, size // 128, 128).transpose(0, 3, 1, 2, 4)
    spread = lax.all_to_all(
        tiles.reshape(everyone, 2, 128), EVERYONE, split_axis=0, concat_axis=0, tiled=True
    )
    outgoing = select_rows(source, spread)
    delivered = lax.all_to_all(outgoing, EVERYONE, split_axis=0, concat_axis=0, tiled=True)
    delivered = delivered.reshape(size // 16, size // 128, 4, 2, 128).transpose(0, 2, 3, 1, 4)
    delivered = delivered.reshape(size // 2, size)

    pieces = [lax.dynamic_index_in_dim(summed, zl, 0, keepdims=False)]
    for step in range(1, zls):
        piece = lax.dynamic_index_in_dim(summed, (zl + step) % zls, 0, keepdims=False)
        route = [(index, (index + step) % zls) for index in range(zls)]
        pieces.append(lax.ppermute(piece, "zl", route))
    pieces = lax.all_gather(jnp.stack(pieces), "core")
    delivered = lax.all_gather(delivered, "core")

    place = jnp.stack([core, zl]).astype(jnp.int32)
    update = precondition(place, delivered, diagonals, pieces)

    update = update.reshape(zls * reps, rows // reps, size)
    arrived = lax.all_to_all(update, ("zl", "rep"), split_axis=0, concat_axis=0, tiled=True)
    return arrived.transpose(1, 0, 2).reshape(rows // reps, width)


def solution(mesh):
    fsdp, reps = mesh.devices.shape
    fine = Mesh(mesh.devices.reshape(4, 4, fsdp // 32, 2, reps), EVERYONE)
    return jax.shard_map(
        on_device,
        mesh=fine,
        in_specs=(P("rep", PLANE, None), P(PLANE, "rep", None, None), P()),
        out_specs=P(EVERYONE, None),
        check_vma=False,
    )
```

```python
import jax
import jax.numpy as jnp
from jax import lax
from jax.experimental import pallas as pl
from jax.experimental.pallas import tpu as pltpu
from jax.sharding import Mesh
from jax.sharding import PartitionSpec as P

POWER_STEPS = 6
EPSILON = 1e-06

PLANE = ("y", "zq", "zl", "core")
EVERYONE = PLANE + ("rep",)
CHIP_ROWS = PLANE[:3]
ACROSS = ("core", "rep") + CHIP_ROWS

BF16 = jnp.bfloat16
F32 = jnp.float32


def matmul(a, b, contract=((1,), (0,))):
    return lax.dot_general(a, b, (contract, ((), ())), preferred_element_type=F32)


def grid_of(shape):
    return (
        lax.broadcasted_iota(jnp.int32, shape, 0),
        lax.broadcasted_iota(jnp.int32, shape, 1),
    )


def pack_kernel(stat_ref, packed_ref, diagonal_ref):
    half = packed_ref.shape[0]
    first, last = stat_ref[:half, :half], stat_ref[half:, half:]
    row, col = grid_of((half, half))
    packed_ref[:, :half] = jnp.where(row <= col, first, last).astype(BF16)
    packed_ref[:, half:] = stat_ref[:half, half:].astype(BF16)
    diagonal_ref[...] = jnp.sum(jnp.where(row == col, last, 0.0), axis=0, keepdims=True)


def pack_statistic(stat):
    size = stat.shape[0]
    vmem = pl.BlockSpec(memory_space=pltpu.VMEM)
    return pl.pallas_call(
        pack_kernel,
        out_shape=[
            jax.ShapeDtypeStruct((size // 2, size), BF16),
            jax.ShapeDtypeStruct((1, size // 2), F32),
        ],
        in_specs=[vmem],
        out_specs=[vmem, vmem],
        compiler_params=pltpu.CompilerParams(vmem_limit_bytes=8 * 2**20),
        name="pack_statistic",
    )(stat)


def parts_kernel(place_ref, partial_ref, *parts_refs):
    zl, rep = place_ref[1], place_ref[2]
    zls, rows, size = parts_refs[0].shape
    reps = len(parts_refs)
    for k in range(reps):
        for i in range(zls):
            block = lax.rem(zl + i, zls) * reps + lax.rem(rep + k, reps)
            columns = pl.ds(pl.multiple_of(block * size, size), size)
            parts_refs[k][i] = partial_ref[0, :, columns]


def part_columns(place, partial, reps, zls, size):
    vmem = pl.BlockSpec(memory_space=pltpu.VMEM)
    return pl.pallas_call(
        parts_kernel,
        out_shape=[jax.ShapeDtypeStruct((zls, partial.shape[1], size), BF16)] * reps,
        in_specs=[pl.BlockSpec(memory_space=pltpu.SMEM), vmem],
        out_specs=[vmem] * reps,
        compiler_params=pltpu.CompilerParams(vmem_limit_bytes=8 * 2**20),
        name="part_columns",
    )(place, partial)


def select_kernel(source_ref, table_ref, diagonal_ref, out_ref):
    lines, lanes = table_ref.shape[1:]
    parts = [diagonal_ref[:, line * lanes : (line + 1) * lanes] for line in range(lines)]
    diagonal = jnp.concatenate(parts, axis=0).astype(BF16)
    wide = table_ref.shape[0] // (out_ref.shape[0] - table_ref.shape[0])

    def body(index, carry):
        for j in range(wide):
            out_ref[index * (wide + 1) + j] = table_ref[source_ref[index * wide + j]]
        out_ref[index * (wide + 1) + wide] = diagonal
        return carry

    lax.fori_loop(0, table_ref.shape[0] // wide, body, 0, unroll=64)


def select_rows(source, table, diagonal, wide):
    count, lines, lanes = table.shape
    vmem = pl.BlockSpec(memory_space=pltpu.VMEM)
    return pl.pallas_call(
        select_kernel,
        out_shape=jax.ShapeDtypeStruct((count + count // wide, lines, lanes), table.dtype),
        in_specs=[pl.BlockSpec(memory_space=pltpu.SMEM), vmem, vmem],
        out_specs=vmem,
        compiler_params=pltpu.CompilerParams(vmem_limit_bytes=8 * 2**20),
        name="select_rows",
    )(source, table, diagonal)


def regroup_kernel(place_ref, source_ref, table_ref, out_ref):
    reps, slots, lines, lanes = out_ref.shape
    wide = 2 * reps
    rows = table_ref.shape[0] // (wide + 1)
    plane, row = place_ref[0] * reps + place_ref[2], place_ref[3]

    def body(index, carry):
        for side in range(2):
            for rep in range(reps):
                piece = table_ref[index * (wide + 1) + side * reps + rep]
                out_ref[rep, side * rows + index] = piece
        return carry

    lax.fori_loop(0, rows, body, 0, unroll=4)
    nothing = jnp.zeros((lines, lanes), F32)
    for rep in range(reps):
        for side in range(2):
            origin = source_ref[row * wide + side * reps + rep]
            piece = table_ref[lax.div(origin, wide) * (wide + 1) + wide].astype(F32)
            here = lax.rem(origin, wide) == plane
            out_ref[rep, 2 * rows + side] = jnp.where(here, piece, nothing).astype(BF16)
        for slot in range(2 * rows + 2, slots):
            out_ref[rep, slot] = nothing.astype(BF16)


def regroup(place, source, table, reps, slots):
    smem = pl.BlockSpec(memory_space=pltpu.SMEM)
    vmem = pl.BlockSpec(memory_space=pltpu.VMEM)
    return pl.pallas_call(
        regroup_kernel,
        out_shape=jax.ShapeDtypeStruct((reps, slots) + table.shape[1:], table.dtype),
        in_specs=[smem, smem, vmem],
        out_specs=vmem,
        compiler_params=pltpu.CompilerParams(vmem_limit_bytes=8 * 2**20),
        name="regroup",
    )(place, source, table)


def unfold(packed, diagonal, stat_ref):
    half = packed.shape[0]
    folded = packed[:, :half].astype(F32)
    cross = packed[:, half:].astype(F32)
    row, col = grid_of((half, half))
    turned = folded.T
    stat_ref[:half, :half] += jnp.where(row <= col, folded, turned)
    lower = jnp.where(row > col, folded, turned)
    stat_ref[half:, half:] += jnp.where(row == col, diagonal, lower)
    stat_ref[:half, half:] += cross
    stat_ref[half:, :half] += cross.T


def main_kernel(place_ref, packed_ref, pieces_ref, out_ref, grad_ref, left_ref, right_ref):
    core, zl = place_ref[0], place_ref[1]
    cores, steps, rows, size = pieces_ref.shape
    for step in range(steps):
        origin = lax.rem(zl - step + steps, steps)
        for member in range(cores):
            first = pl.multiple_of((origin * cores + member) * rows, rows)
            grad_ref[pl.ds(first, rows), :] = pieces_ref[member, step]
    gradient = grad_ref[...]
    left_ref[...] = matmul(gradient, gradient, ((1,), (1,)))
    right_ref[...] = matmul(gradient.T, gradient)
    planes = [(member, rep) for member in range(cores) for rep in range(packed_ref.shape[1])]
    part = size // 2 // len(planes)
    diagonals = sum(packed_ref[m, r, 2 * part : 2 * part + 16, :].astype(F32) for m, r in planes)
    for side, ref in enumerate((left_ref, right_ref)):
        packed = [packed_ref[m, r, side * part : (side + 1) * part, :] for m, r in planes]
        lines = [diagonals[2 * side + line : 2 * side + line + 1, : size // 4] for line in range(2)]
        unfold(jnp.concatenate(packed, axis=0), jnp.concatenate(lines, axis=1), ref)
    roots = []
    row, col = grid_of((size, size))
    identity = jnp.where(row == col, 1.0, 0.0)
    images = [jnp.sum(ref[...], axis=0, keepdims=True) for ref in (left_ref, right_ref)]
    for power_step in range(POWER_STEPS):
        axis = 1 - power_step % 2
        scales = [lax.rsqrt(jnp.sum(image * image) + EPSILON) for image in images]
        vectors = images
        images = [
            jnp.sum(ref[...] * vector, axis=axis, keepdims=True) * scale
            for ref, vector, scale in zip((left_ref, right_ref), vectors, scales)
        ]
    vectors = [vector * scale for vector, scale in zip(vectors, scales)]
    for ref, vector, image in zip((left_ref, right_ref), vectors, images):
        turned = jnp.sum(identity * vector, axis=0, keepdims=True)
        largest = jnp.sum(turned * image)
        scaled = ref[...] * (1.0 / largest)
        narrow = scaled.astype(BF16)
        second = matmul(narrow, narrow)
        times = 1.25 * scaled - 0.25 * second
        square = 1.5625 * identity - 0.3125 * scaled - 0.25 * times
        times = times.astype(BF16)
        narrow = square.astype(BF16)
        fourth = matmul(narrow, narrow).astype(BF16)
        last = matmul(fourth, times)
        roots.append((25.0 / 16.0) * identity - (5.0 / 16.0) * scaled - 0.25 * last)
    left, right = roots
    half_way = matmul(left.astype(BF16), gradient)
    raw = matmul(half_way.astype(BF16), right.astype(BF16))
    wide = gradient.astype(F32)
    scale = jnp.sqrt(jnp.sum(wide * wide) + EPSILON) * lax.rsqrt(
        jnp.sum(raw * raw) + EPSILON
    )
    left_ref[...] = raw
    for origin in range(steps):
        first = pl.multiple_of(origin * cores * rows + core * rows, rows)
        out_ref[origin] = (left_ref[pl.ds(first, rows), :] * scale).astype(BF16)


def precondition(place, packed, pieces):
    size = pieces.shape[-1]
    vmem = pl.BlockSpec(memory_space=pltpu.VMEM)
    return pl.pallas_call(
        main_kernel,
        out_shape=jax.ShapeDtypeStruct(pieces.shape[1:], BF16),
        in_specs=[pl.BlockSpec(memory_space=pltpu.SMEM), vmem, vmem],
        out_specs=vmem,
        scratch_shapes=[
            pltpu.VMEM((size, size), BF16),
            pltpu.VMEM((size, size), F32),
            pltpu.VMEM((size, size), F32),
        ],
        compiler_params=pltpu.CompilerParams(vmem_limit_bytes=40 * 2**20),
        name="precondition",
    )(place, packed, pieces)


def on_device(partials, factor_stats, owner_slots):
    rows, width = partials.shape[1:]
    size = factor_stats.shape[-1]
    reps, zls, cores = (lax.axis_size(name) for name in ("rep", "zl", "core"))
    core, zl, rep = (lax.axis_index(name) for name in ("core", "zl", "rep"))
    plane = cores * reps
    place = jnp.stack([core, zl, rep, lax.axis_index(CHIP_ROWS)]).astype(jnp.int32)

    source = 2 * owner_slots.reshape(-1, 1, reps) + jnp.arange(2, dtype=jnp.int32)[None, :, None]
    source = source.reshape(-1)
    everyone = source.shape[0]

    parts = list(part_columns(place, partials, reps, zls, size))
    for step in range(1, reps):
        route = [(index, (index + step) % reps) for index in range(reps)]
        parts[step] = lax.ppermute(parts[step], "rep", route)

    packed, diagonal = pack_statistic(factor_stats[0, 0])
    tiles = packed.reshape(size // 16, 4, 2, size // 128, 128).transpose(0, 3, 1, 2, 4)
    spread = lax.all_to_all(
        tiles.reshape(everyone, 2, 128), ACROSS, split_axis=0, concat_axis=0, tiled=True
    )
    spread, parts = lax.optimization_barrier((spread, parts))
    arrival = source % plane * (everyone // plane) + source // plane
    outgoing = select_rows(arrival, spread, diagonal, plane)
    in_row = lax.all_to_all(outgoing, CHIP_ROWS, split_axis=0, concat_axis=0, tiled=True)

    summed = sum(part.astype(F32) for part in parts).astype(BF16)
    pieces = [summed[0]]
    for step in range(1, zls):
        route = [(index, (index + step) % zls) for index in range(zls)]
        pieces.append(lax.ppermute(summed[step], "zl", route))
    pieces = lax.all_gather(jnp.stack(pieces), "core")
    in_row, pieces = lax.optimization_barrier((in_row, pieces))

    slots = 2 * everyone // plane + 32
    outgoing = regroup(place, source, in_row, reps, slots)
    delivered = lax.all_to_all(outgoing, "rep", split_axis=0, concat_axis=0, tiled=True)
    delivered = delivered.reshape(reps, slots // 16, size // 128, 4, 2, 128)
    delivered = delivered.transpose(0, 1, 3, 4, 2, 5).reshape(reps, slots // 2, size)
    delivered = lax.all_gather(delivered, "core")
    update = precondition(place, delivered, pieces)

    update = update.reshape(zls * reps, rows // reps, size)
    arrived = lax.all_to_all(update, ("zl", "rep"), split_axis=0, concat_axis=0, tiled=True)
    return arrived.transpose(1, 0, 2).reshape(rows // reps, width)


def solution(mesh):
    fsdp, reps = mesh.devices.shape
    fine = Mesh(mesh.devices.reshape(4, 4, fsdp // 32, 2, reps), EVERYONE)
    return jax.shard_map(
        on_device,
        mesh=fine,
        in_specs=(P("rep", PLANE, None), P(PLANE, "rep", None, None), P()),
        out_specs=P(EVERYONE, None),
        check_vma=False,
    )
```

```python
import jax
import jax.numpy as jnp
from jax import lax
from jax.experimental import pallas as pl
from jax.experimental.pallas import tpu as pltpu
from jax.sharding import Mesh
from jax.sharding import PartitionSpec as P

POWER_STEPS = 6
EPSILON = 1e-06

PLANE = ("y", "zq", "zl", "core")
EVERYONE = PLANE + ("rep",)
CHIP_ROWS = PLANE[:3]
ACROSS = ("core", "rep") + CHIP_ROWS

BF16 = jnp.bfloat16
F32 = jnp.float32


def matmul(a, b, contract=((1,), (0,))):
    return lax.dot_general(a, b, (contract, ((), ())), preferred_element_type=F32)


def grid_of(shape):
    return (
        lax.broadcasted_iota(jnp.int32, shape, 0),
        lax.broadcasted_iota(jnp.int32, shape, 1),
    )


def pack_kernel(stat_ref, packed_ref, diagonal_ref):
    half = packed_ref.shape[0]
    first, last = stat_ref[:half, :half], stat_ref[half:, half:]
    row, col = grid_of((half, half))
    packed_ref[:, :half] = jnp.where(row <= col, first, last).astype(BF16)
    packed_ref[:, half:] = stat_ref[:half, half:].astype(BF16)
    diagonal_ref[...] = jnp.sum(jnp.where(row == col, last, 0.0), axis=0, keepdims=True)


def pack_statistic(stat):
    size = stat.shape[0]
    vmem = pl.BlockSpec(memory_space=pltpu.VMEM)
    return pl.pallas_call(
        pack_kernel,
        out_shape=[
            jax.ShapeDtypeStruct((size // 2, size), BF16),
            jax.ShapeDtypeStruct((1, size // 2), F32),
        ],
        in_specs=[vmem],
        out_specs=[vmem, vmem],
        compiler_params=pltpu.CompilerParams(vmem_limit_bytes=8 * 2**20),
        name="pack_statistic",
    )(stat)


def parts_kernel(place_ref, partial_ref, *parts_refs):
    zl, rep = place_ref[1], place_ref[2]
    zls, rows, size = parts_refs[0].shape
    reps = len(parts_refs)
    for k in range(reps):
        for i in range(zls):
            block = lax.rem(zl + i, zls) * reps + lax.rem(rep + k, reps)
            columns = pl.ds(pl.multiple_of(block * size, size), size)
            parts_refs[k][i] = partial_ref[0, :, columns]


def part_columns(place, partial, reps, zls, size):
    vmem = pl.BlockSpec(memory_space=pltpu.VMEM)
    return pl.pallas_call(
        parts_kernel,
        out_shape=[jax.ShapeDtypeStruct((zls, partial.shape[1], size), BF16)] * reps,
        in_specs=[pl.BlockSpec(memory_space=pltpu.SMEM), vmem],
        out_specs=[vmem] * reps,
        compiler_params=pltpu.CompilerParams(vmem_limit_bytes=8 * 2**20),
        name="part_columns",
    )(place, partial)


def select_kernel(source_ref, table_ref, diagonal_ref, out_ref):
    lines, lanes = table_ref.shape[1:]
    parts = [diagonal_ref[:, line * lanes : (line + 1) * lanes] for line in range(lines)]
    diagonal = jnp.concatenate(parts, axis=0).astype(BF16)
    wide = table_ref.shape[0] // (out_ref.shape[0] - table_ref.shape[0])

    def body(index, carry):
        for j in range(wide):
            out_ref[index * (wide + 1) + j] = table_ref[source_ref[index * wide + j]]
        out_ref[index * (wide + 1) + wide] = diagonal
        return carry

    lax.fori_loop(0, table_ref.shape[0] // wide, body, 0, unroll=64)


def select_rows(source, table, diagonal, wide):
    count, lines, lanes = table.shape
    vmem = pl.BlockSpec(memory_space=pltpu.VMEM)
    return pl.pallas_call(
        select_kernel,
        out_shape=jax.ShapeDtypeStruct((count + count // wide, lines, lanes), table.dtype),
        in_specs=[pl.BlockSpec(memory_space=pltpu.SMEM), vmem, vmem],
        out_specs=vmem,
        compiler_params=pltpu.CompilerParams(vmem_limit_bytes=8 * 2**20),
        name="select_rows",
    )(source, table, diagonal)


def regroup_kernel(place_ref, source_ref, table_ref, out_ref):
    reps, slots, lines, lanes = out_ref.shape
    wide = 2 * reps
    rows = table_ref.shape[0] // (wide + 1)
    plane, row = place_ref[0] * reps + place_ref[2], place_ref[3]

    def body(index, carry):
        for side in range(2):
            for rep in range(reps):
                piece = table_ref[index * (wide + 1) + side * reps + rep]
                out_ref[rep, side * rows + index] = piece
        return carry

    lax.fori_loop(0, rows, body, 0, unroll=4)
    nothing = jnp.zeros((lines, lanes), F32)
    for rep in range(reps):
        for side in range(2):
            origin = source_ref[row * wide + side * reps + rep]
            piece = table_ref[lax.div(origin, wide) * (wide + 1) + wide].astype(F32)
            here = lax.rem(origin, wide) == plane
            out_ref[rep, 2 * rows + side] = jnp.where(here, piece, nothing).astype(BF16)
        for slot in range(2 * rows + 2, slots):
            out_ref[rep, slot] = nothing.astype(BF16)


def regroup(place, source, table, reps, slots):
    smem = pl.BlockSpec(memory_space=pltpu.SMEM)
    vmem = pl.BlockSpec(memory_space=pltpu.VMEM)
    return pl.pallas_call(
        regroup_kernel,
        out_shape=jax.ShapeDtypeStruct((reps, slots) + table.shape[1:], table.dtype),
        in_specs=[smem, smem, vmem],
        out_specs=vmem,
        compiler_params=pltpu.CompilerParams(vmem_limit_bytes=8 * 2**20),
        name="regroup",
    )(place, source, table)


def unfold(packed, diagonal, stat_ref):
    half = packed.shape[0]
    folded = packed[:, :half].astype(F32)
    cross = packed[:, half:].astype(F32)
    row, col = grid_of((half, half))
    turned = folded.T
    stat_ref[:half, :half] += jnp.where(row <= col, folded, turned)
    lower = jnp.where(row > col, folded, turned)
    stat_ref[half:, half:] += jnp.where(row == col, diagonal, lower)
    stat_ref[:half, half:] += cross
    stat_ref[half:, :half] += cross.T


def main_kernel(place_ref, packed_ref, pieces_ref, out_ref, grad_ref, left_ref, right_ref):
    core, zl = place_ref[0], place_ref[1]
    cores, steps, rows, size = pieces_ref.shape
    for step in range(steps):
        origin = lax.rem(zl - step + steps, steps)
        for member in range(cores):
            first = pl.multiple_of((origin * cores + member) * rows, rows)
            grad_ref[pl.ds(first, rows), :] = pieces_ref[member, step]
    gradient = grad_ref[...]
    left_ref[...] = matmul(gradient, gradient, ((1,), (1,)))
    right_ref[...] = matmul(gradient.T, gradient)
    planes = [(member, rep) for member in range(cores) for rep in range(packed_ref.shape[1])]
    part = size // 2 // len(planes)
    diagonals = sum(packed_ref[m, r, 2 * part : 2 * part + 16, :].astype(F32) for m, r in planes)
    for side, ref in enumerate((left_ref, right_ref)):
        packed = [packed_ref[m, r, side * part : (side + 1) * part, :] for m, r in planes]
        lines = [diagonals[2 * side + line : 2 * side + line + 1, : size // 4] for line in range(2)]
        unfold(jnp.concatenate(packed, axis=0), jnp.concatenate(lines, axis=1), ref)
    roots = []
    row, col = grid_of((size, size))
    identity = jnp.where(row == col, 1.0, 0.0)
    images = [jnp.sum(ref[...], axis=0, keepdims=True) for ref in (left_ref, right_ref)]
    for power_step in range(POWER_STEPS):
        axis = 1 - power_step % 2
        scales = [lax.rsqrt(jnp.sum(image * image) + EPSILON) for image in images]
        vectors = images
        images = [
            jnp.sum(ref[...] * vector, axis=axis, keepdims=True) * scale
            for ref, vector, scale in zip((left_ref, right_ref), vectors, scales)
        ]
    vectors = [vector * scale for vector, scale in zip(vectors, scales)]
    for ref, vector, image in zip((left_ref, right_ref), vectors, images):
        turned = jnp.sum(identity * vector, axis=0, keepdims=True)
        largest = jnp.sum(turned * image)
        scaled = ref[...] * (1.0 / largest)
        narrow = scaled.astype(BF16)
        second = matmul(narrow, narrow)
        times = 1.25 * scaled - 0.25 * second
        square = 1.5625 * identity - 0.3125 * scaled - 0.25 * times
        times = times.astype(BF16)
        narrow = square.astype(BF16)
        fourth = matmul(narrow, narrow).astype(BF16)
        last = matmul(fourth, times)
        roots.append((25.0 / 16.0) * identity - (5.0 / 16.0) * scaled - 0.25 * last)
    left, right = roots
    half_way = matmul(left.astype(BF16), gradient)
    raw = matmul(half_way.astype(BF16), right.astype(BF16))
    wide = gradient.astype(F32)
    scale = jnp.sqrt(jnp.sum(wide * wide) + EPSILON) * lax.rsqrt(
        jnp.sum(raw * raw) + EPSILON
    )
    left_ref[...] = raw
    for origin in range(steps):
        first = pl.multiple_of(origin * cores * rows + core * rows, rows)
        out_ref[origin] = (left_ref[pl.ds(first, rows), :] * scale).astype(BF16)


def precondition(place, packed, pieces):
    size = pieces.shape[-1]
    vmem = pl.BlockSpec(memory_space=pltpu.VMEM)
    return pl.pallas_call(
        main_kernel,
        out_shape=jax.ShapeDtypeStruct(pieces.shape[1:], BF16),
        in_specs=[pl.BlockSpec(memory_space=pltpu.SMEM), vmem, vmem],
        out_specs=vmem,
        scratch_shapes=[
            pltpu.VMEM((size, size), BF16),
            pltpu.VMEM((size, size), F32),
            pltpu.VMEM((size, size), F32),
        ],
        compiler_params=pltpu.CompilerParams(vmem_limit_bytes=40 * 2**20),
        name="precondition",
    )(place, packed, pieces)


def on_device(partials, factor_stats, owner_slots):
    rows, width = partials.shape[1:]
    size = factor_stats.shape[-1]
    reps, zls, cores = (lax.axis_size(name) for name in ("rep", "zl", "core"))
    core, zl, rep = (lax.axis_index(name) for name in ("core", "zl", "rep"))
    plane = cores * reps
    place = jnp.stack([core, zl, rep, lax.axis_index(CHIP_ROWS)]).astype(jnp.int32)

    source = 2 * owner_slots.reshape(-1, 1, reps) + jnp.arange(2, dtype=jnp.int32)[None, :, None]
    source = source.reshape(-1)
    everyone = source.shape[0]

    parts = list(part_columns(place, partials, reps, zls, size))
    for step in range(1, reps):
        route = [(index, (index + step) % reps) for index in range(reps)]
        parts[step] = lax.ppermute(parts[step], "rep", route)

    packed, diagonal = pack_statistic(factor_stats[0, 0])
    tiles = packed.reshape(size // 16, 4, 2, size // 128, 128).transpose(0, 3, 1, 2, 4)
    spread = lax.all_to_all(
        tiles.reshape(everyone, 2, 128), ACROSS, split_axis=0, concat_axis=0, tiled=True
    )
    spread, parts[1], parts[3] = lax.optimization_barrier((spread, parts[1], parts[3]))
    arrival = source % plane * (everyone // plane) + source // plane
    outgoing = select_rows(arrival, spread, diagonal, plane)
    in_row = lax.all_to_all(outgoing, CHIP_ROWS, split_axis=0, concat_axis=0, tiled=True)

    summed = sum(part.astype(F32) for part in parts).astype(BF16)
    pieces = [summed[0]]
    for step in range(1, zls):
        route = [(index, (index + step) % zls) for index in range(zls)]
        pieces.append(lax.ppermute(summed[step], "zl", route))
    in_row, pieces[1] = lax.optimization_barrier((in_row, pieces[1]))
    pieces = lax.all_gather(jnp.stack(pieces), "core")

    slots = 2 * everyone // plane + 32
    outgoing = regroup(place, source, in_row, reps, slots)
    delivered = lax.all_to_all(outgoing, "rep", split_axis=0, concat_axis=0, tiled=True)
    delivered = delivered.reshape(reps, slots // 16, size // 128, 4, 2, 128)
    delivered = delivered.transpose(0, 1, 3, 4, 2, 5).reshape(reps, slots // 2, size)
    delivered = lax.all_gather(delivered, "core")
    update = precondition(place, delivered, pieces)

    update = update.reshape(zls * reps, rows // reps, size)
    arrived = lax.all_to_all(update, ("zl", "rep"), split_axis=0, concat_axis=0, tiled=True)
    return arrived.transpose(1, 0, 2).reshape(rows // reps, width)


def solution(mesh):
    fsdp, reps = mesh.devices.shape
    fine = Mesh(mesh.devices.reshape(4, 4, fsdp // 32, 2, reps), EVERYONE)
    return jax.shard_map(
        on_device,
        mesh=fine,
        in_specs=(P("rep", PLANE, None), P(PLANE, "rep", None, None), P()),
        out_specs=P(EVERYONE, None),
        check_vma=False,
    )
```

```python
import jax
import jax.numpy as jnp
from jax import lax
from jax.experimental import pallas as pl
from jax.experimental.pallas import tpu as pltpu
from jax.sharding import Mesh
from jax.sharding import PartitionSpec as P

POWER_STEPS = 6
EPSILON = 1e-06

PLANE = ("y", "zq", "zl", "core")
EVERYONE = PLANE + ("rep",)
CHIP_ROWS = PLANE[:3]
ACROSS = ("core", "rep") + CHIP_ROWS

BF16 = jnp.bfloat16
F32 = jnp.float32


def matmul(a, b, contract=((1,), (0,))):
    return lax.dot_general(a, b, (contract, ((), ())), preferred_element_type=F32)


def grid_of(shape):
    return (
        lax.broadcasted_iota(jnp.int32, shape, 0),
        lax.broadcasted_iota(jnp.int32, shape, 1),
    )


def pack_kernel(stat_ref, packed_ref, diagonal_ref):
    half = packed_ref.shape[0]
    first, last = stat_ref[:half, :half], stat_ref[half:, half:]
    row, col = grid_of((half, half))
    packed_ref[:, :half] = jnp.where(row <= col, first, last).astype(BF16)
    packed_ref[:, half:] = stat_ref[:half, half:].astype(BF16)
    diagonal_ref[...] = jnp.sum(jnp.where(row == col, last, 0.0), axis=0, keepdims=True)


def pack_statistic(stat):
    size = stat.shape[0]
    vmem = pl.BlockSpec(memory_space=pltpu.VMEM)
    return pl.pallas_call(
        pack_kernel,
        out_shape=[
            jax.ShapeDtypeStruct((size // 2, size), BF16),
            jax.ShapeDtypeStruct((1, size // 2), F32),
        ],
        in_specs=[vmem],
        out_specs=[vmem, vmem],
        compiler_params=pltpu.CompilerParams(vmem_limit_bytes=8 * 2**20),
        name="pack_statistic",
    )(stat)


def parts_kernel(place_ref, partial_ref, *parts_refs):
    zl, rep = place_ref[1], place_ref[2]
    zls, rows, size = parts_refs[0].shape
    reps = len(parts_refs)
    for k in range(reps):
        for i in range(zls):
            block = lax.rem(zl + i, zls) * reps + lax.rem(rep + k, reps)
            columns = pl.ds(pl.multiple_of(block * size, size), size)
            parts_refs[k][i] = partial_ref[0, :, columns]


def part_columns(place, partial, reps, zls, size):
    vmem = pl.BlockSpec(memory_space=pltpu.VMEM)
    return pl.pallas_call(
        parts_kernel,
        out_shape=[jax.ShapeDtypeStruct((zls, partial.shape[1], size), BF16)] * reps,
        in_specs=[pl.BlockSpec(memory_space=pltpu.SMEM), vmem],
        out_specs=[vmem] * reps,
        compiler_params=pltpu.CompilerParams(vmem_limit_bytes=8 * 2**20),
        name="part_columns",
    )(place, partial)


def select_kernel(source_ref, table_ref, diagonal_ref, out_ref):
    lines, lanes = table_ref.shape[1:]
    parts = [diagonal_ref[:, line * lanes : (line + 1) * lanes] for line in range(lines)]
    diagonal = jnp.concatenate(parts, axis=0).astype(BF16)
    wide = table_ref.shape[0] // (out_ref.shape[0] - table_ref.shape[0])

    def body(index, carry):
        for j in range(wide):
            out_ref[index * (wide + 1) + j] = table_ref[source_ref[index * wide + j]]
        out_ref[index * (wide + 1) + wide] = diagonal
        return carry

    lax.fori_loop(0, table_ref.shape[0] // wide, body, 0, unroll=64)


def select_rows(source, table, diagonal, wide):
    count, lines, lanes = table.shape
    vmem = pl.BlockSpec(memory_space=pltpu.VMEM)
    return pl.pallas_call(
        select_kernel,
        out_shape=jax.ShapeDtypeStruct((count + count // wide, lines, lanes), table.dtype),
        in_specs=[pl.BlockSpec(memory_space=pltpu.SMEM), vmem, vmem],
        out_specs=vmem,
        compiler_params=pltpu.CompilerParams(vmem_limit_bytes=8 * 2**20),
        name="select_rows",
    )(source, table, diagonal)


def regroup_kernel(place_ref, source_ref, table_ref, out_ref):
    reps, slots, lines, lanes = out_ref.shape
    wide = 2 * reps
    rows = table_ref.shape[0] // (wide + 1)
    plane, row = place_ref[0] * reps + place_ref[2], place_ref[3]

    def body(index, carry):
        for side in range(2):
            for rep in range(reps):
                piece = table_ref[index * (wide + 1) + side * reps + rep]
                out_ref[rep, side * rows + index] = piece
        return carry

    lax.fori_loop(0, rows, body, 0, unroll=4)
    nothing = jnp.zeros((lines, lanes), F32)
    for rep in range(reps):
        for side in range(2):
            origin = source_ref[row * wide + side * reps + rep]
            piece = table_ref[lax.div(origin, wide) * (wide + 1) + wide].astype(F32)
            here = lax.rem(origin, wide) == plane
            out_ref[rep, 2 * rows + side] = jnp.where(here, piece, nothing).astype(BF16)
        for slot in range(2 * rows + 2, slots):
            out_ref[rep, slot] = nothing.astype(BF16)


def regroup(place, source, table, reps, slots):
    smem = pl.BlockSpec(memory_space=pltpu.SMEM)
    vmem = pl.BlockSpec(memory_space=pltpu.VMEM)
    return pl.pallas_call(
        regroup_kernel,
        out_shape=jax.ShapeDtypeStruct((reps, slots) + table.shape[1:], table.dtype),
        in_specs=[smem, smem, vmem],
        out_specs=vmem,
        compiler_params=pltpu.CompilerParams(vmem_limit_bytes=8 * 2**20),
        name="regroup",
    )(place, source, table)


def unfold(packed, diagonal, stat_ref):
    half = packed.shape[0]
    folded = packed[:, :half].astype(F32)
    cross = packed[:, half:].astype(F32)
    row, col = grid_of((half, half))
    turned = folded.T
    stat_ref[:half, :half] += jnp.where(row <= col, folded, turned)
    lower = jnp.where(row > col, folded, turned)
    stat_ref[half:, half:] += jnp.where(row == col, diagonal, lower)
    stat_ref[:half, half:] += cross
    stat_ref[half:, :half] += cross.T


def main_kernel(place_ref, packed_ref, pieces_ref, out_ref, grad_ref, left_ref, right_ref):
    core, zl = place_ref[0], place_ref[1]
    cores, steps, rows, size = pieces_ref.shape
    for step in range(steps):
        origin = lax.rem(zl - step + steps, steps)
        for member in range(cores):
            first = pl.multiple_of((origin * cores + member) * rows, rows)
            grad_ref[pl.ds(first, rows), :] = pieces_ref[member, step]
    gradient = grad_ref[...]
    left_ref[...] = matmul(gradient, gradient, ((1,), (1,)))
    right_ref[...] = matmul(gradient.T, gradient)
    planes = [(member, rep) for member in range(cores) for rep in range(packed_ref.shape[1])]
    part = size // 2 // len(planes)
    diagonals = sum(packed_ref[m, r].astype(F32)[2 * part :, : size // 4] for m, r in planes)
    for side, ref in enumerate((left_ref, right_ref)):
        packed = [packed_ref[m, r, side * part : (side + 1) * part, :] for m, r in planes]
        lines = [diagonals[2 * side + line : 2 * side + line + 1, :] for line in range(2)]
        unfold(jnp.concatenate(packed, axis=0), jnp.concatenate(lines, axis=1), ref)
    row, col = grid_of((size, size))
    identity = jnp.where(row == col, 1.0, 0.0)
    images = [jnp.sum(ref[...], axis=0, keepdims=True) for ref in (left_ref, right_ref)]
    for power_step in range(POWER_STEPS):
        axis = 1 - power_step % 2
        scales = [lax.rsqrt(jnp.sum(image * image) + EPSILON) for image in images]
        vectors = images
        images = [
            jnp.sum(ref[...] * vector, axis=axis, keepdims=True) * scale
            for ref, vector, scale in zip((left_ref, right_ref), vectors, scales)
        ]
    vectors = [vector * scale for vector, scale in zip(vectors, scales)]
    scaleds = []
    for ref, vector, image in zip((left_ref, right_ref), vectors, images):
        turned = jnp.sum(identity * vector, axis=0, keepdims=True)
        scaleds.append(ref[...] * (1.0 / jnp.sum(turned * image)))
    narrows = [scaled.astype(BF16) for scaled in scaleds]
    times = [1.25 * scaled - 0.25 * matmul(n, n) for scaled, n in zip(scaleds, narrows)]
    squares = [
        (1.5625 * identity - 0.3125 * scaled - 0.25 * t).astype(BF16)
        for scaled, t in zip(scaleds, times)
    ]
    fourths = [matmul(square, square).astype(BF16) for square in squares]
    lasts = [matmul(fourth, t.astype(BF16)) for fourth, t in zip(fourths, times)]
    roots = [
        1.5625 * identity - 0.3125 * scaled - 0.25 * last for scaled, last in zip(scaleds, lasts)
    ]
    left, right = roots
    half_way = matmul(left.astype(BF16), gradient)
    raw = matmul(half_way.astype(BF16), right.astype(BF16))
    wide = gradient.astype(F32)
    scale = jnp.sqrt(jnp.sum(wide * wide) + EPSILON) * lax.rsqrt(
        jnp.sum(raw * raw) + EPSILON
    )
    left_ref[...] = raw
    for origin in range(steps):
        first = pl.multiple_of(origin * cores * rows + core * rows, rows)
        out_ref[origin] = (left_ref[pl.ds(first, rows), :] * scale).astype(BF16)


def precondition(place, packed, pieces):
    size = pieces.shape[-1]
    vmem = pl.BlockSpec(memory_space=pltpu.VMEM)
    return pl.pallas_call(
        main_kernel,
        out_shape=jax.ShapeDtypeStruct(pieces.shape[1:], BF16),
        in_specs=[pl.BlockSpec(memory_space=pltpu.SMEM), vmem, vmem],
        out_specs=vmem,
        scratch_shapes=[
            pltpu.VMEM((size, size), BF16),
            pltpu.VMEM((size, size), F32),
            pltpu.VMEM((size, size), F32),
        ],
        compiler_params=pltpu.CompilerParams(vmem_limit_bytes=40 * 2**20),
        name="precondition",
    )(place, packed, pieces)


def on_device(partials, factor_stats, owner_slots):
    rows, width = partials.shape[1:]
    size = factor_stats.shape[-1]
    reps, zls, cores = (lax.axis_size(name) for name in ("rep", "zl", "core"))
    core, zl, rep = (lax.axis_index(name) for name in ("core", "zl", "rep"))
    plane = cores * reps
    place = jnp.stack([core, zl, rep, lax.axis_index(CHIP_ROWS)]).astype(jnp.int32)

    source = 2 * owner_slots.reshape(-1, 1, reps) + jnp.arange(2, dtype=jnp.int32)[None, :, None]
    source = source.reshape(-1)
    everyone = source.shape[0]

    parts = list(part_columns(place, partials, reps, zls, size))
    for step in range(1, reps):
        route = [(index, (index + step) % reps) for index in range(reps)]
        parts[step] = lax.ppermute(parts[step], "rep", route)

    packed, diagonal = pack_statistic(factor_stats[0, 0])
    tiles = packed.reshape(size // 16, 4, 2, size // 128, 128).transpose(0, 3, 1, 2, 4)
    spread = lax.all_to_all(
        tiles.reshape(everyone, 2, 128), ACROSS, split_axis=0, concat_axis=0, tiled=True
    )
    spread, parts[1], parts[3] = lax.optimization_barrier((spread, parts[1], parts[3]))
    arrival = source % plane * (everyone // plane) + source // plane
    outgoing = select_rows(arrival, spread, diagonal, plane)
    in_row = lax.all_to_all(outgoing, CHIP_ROWS, split_axis=0, concat_axis=0, tiled=True)

    summed = sum(part.astype(F32) for part in parts).astype(BF16)
    pieces = [summed[0]]
    for step in range(1, zls):
        route = [(index, (index + step) % zls) for index in range(zls)]
        pieces.append(lax.ppermute(summed[step], "zl", route))
    in_row, pieces[1] = lax.optimization_barrier((in_row, pieces[1]))
    pieces = lax.all_gather(jnp.stack(pieces), "core")

    slots = 2 * everyone // plane + 16
    outgoing = regroup(place, source, in_row, reps, slots)
    delivered = lax.all_to_all(outgoing, "rep", split_axis=0, concat_axis=0, tiled=True)
    delivered = delivered.reshape(reps, slots // 16, size // 128, 4, 2, 128)
    delivered = delivered.transpose(0, 1, 3, 4, 2, 5).reshape(reps, slots // 2, size)
    delivered = lax.all_gather(delivered, "core")
    update = precondition(place, delivered, pieces)

    update = update.reshape(zls * reps, rows // reps, size)
    arrived = lax.all_to_all(update, ("zl", "rep"), split_axis=0, concat_axis=0, tiled=True)
    return arrived.transpose(1, 0, 2).reshape(rows // reps, width)


def solution(mesh):
    fsdp, reps = mesh.devices.shape
    fine = Mesh(mesh.devices.reshape(4, 4, fsdp // 32, 2, reps), EVERYONE)
    return jax.shard_map(
        on_device,
        mesh=fine,
        in_specs=(P("rep", PLANE, None), P(PLANE, "rep", None, None), P()),
        out_specs=P(EVERYONE, None),
        check_vma=False,
    )
```

```python
import jax
import jax.numpy as jnp
from jax import lax
from jax.experimental import pallas as pl
from jax.experimental.pallas import tpu as pltpu
from jax.sharding import Mesh
from jax.sharding import PartitionSpec as P

POWER_STEPS = 6
EPSILON = 1e-06

PLANE = ("y", "zq", "zl", "core")
EVERYONE = PLANE + ("rep",)
CHIP_ROWS = PLANE[:3]
ACROSS = ("core", "rep") + CHIP_ROWS

BF16 = jnp.bfloat16
F32 = jnp.float32


def matmul(a, b, contract=((1,), (0,))):
    return lax.dot_general(a, b, (contract, ((), ())), preferred_element_type=F32)


def grid_of(shape):
    return (
        lax.broadcasted_iota(jnp.int32, shape, 0),
        lax.broadcasted_iota(jnp.int32, shape, 1),
    )


def pack_kernel(stat_ref, packed_ref, diagonal_ref):
    half = packed_ref.shape[0]
    first, last = stat_ref[:half, :half], stat_ref[half:, half:]
    row, col = grid_of((half, half))
    packed_ref[:, :half] = jnp.where(row <= col, first, last).astype(BF16)
    packed_ref[:, half:] = stat_ref[:half, half:].astype(BF16)
    diagonal_ref[...] = jnp.sum(jnp.where(row == col, last, 0.0), axis=0, keepdims=True)


def pack_statistic(stat):
    size = stat.shape[0]
    vmem = pl.BlockSpec(memory_space=pltpu.VMEM)
    return pl.pallas_call(
        pack_kernel,
        out_shape=[
            jax.ShapeDtypeStruct((size // 2, size), BF16),
            jax.ShapeDtypeStruct((1, size // 2), F32),
        ],
        in_specs=[vmem],
        out_specs=[vmem, vmem],
        compiler_params=pltpu.CompilerParams(vmem_limit_bytes=8 * 2**20),
        name="pack_statistic",
    )(stat)


def parts_kernel(place_ref, partial_ref, *parts_refs):
    zl, rep = place_ref[1], place_ref[2]
    zls, rows, size = parts_refs[0].shape
    reps = len(parts_refs)
    for k in range(reps):
        for i in range(zls):
            block = lax.rem(zl + i, zls) * reps + lax.rem(rep + k, reps)
            columns = pl.ds(pl.multiple_of(block * size, size), size)
            parts_refs[k][i] = partial_ref[0, :, columns]


def part_columns(place, partial, reps, zls, size):
    vmem = pl.BlockSpec(memory_space=pltpu.VMEM)
    return pl.pallas_call(
        parts_kernel,
        out_shape=[jax.ShapeDtypeStruct((zls, partial.shape[1], size), BF16)] * reps,
        in_specs=[pl.BlockSpec(memory_space=pltpu.SMEM), vmem],
        out_specs=[vmem] * reps,
        compiler_params=pltpu.CompilerParams(vmem_limit_bytes=8 * 2**20),
        name="part_columns",
    )(place, partial)


def select_kernel(source_ref, table_ref, diagonal_ref, out_ref):
    lines, lanes = table_ref.shape[1:]
    parts = [diagonal_ref[:, line * lanes : (line + 1) * lanes] for line in range(lines)]
    diagonal = jnp.concatenate(parts, axis=0).astype(BF16)
    wide = table_ref.shape[0] // (out_ref.shape[0] - table_ref.shape[0])

    def body(index, carry):
        for j in range(wide):
            out_ref[index * (wide + 1) + j] = table_ref[source_ref[index * wide + j]]
        out_ref[index * (wide + 1) + wide] = diagonal
        return carry

    lax.fori_loop(0, table_ref.shape[0] // wide, body, 0, unroll=64)


def select_rows(source, table, diagonal, wide):
    count, lines, lanes = table.shape
    vmem = pl.BlockSpec(memory_space=pltpu.VMEM)
    return pl.pallas_call(
        select_kernel,
        out_shape=jax.ShapeDtypeStruct((count + count // wide, lines, lanes), table.dtype),
        in_specs=[pl.BlockSpec(memory_space=pltpu.SMEM), vmem, vmem],
        out_specs=vmem,
        compiler_params=pltpu.CompilerParams(vmem_limit_bytes=8 * 2**20),
        name="select_rows",
    )(source, table, diagonal)


def regroup_kernel(place_ref, source_ref, table_ref, out_ref):
    reps, slots, lines, lanes = out_ref.shape
    wide = 2 * reps
    rows = table_ref.shape[0] // (wide + 1)
    plane, row = place_ref[0] * reps + place_ref[2], place_ref[3]

    def body(index, carry):
        for side in range(2):
            for rep in range(reps):
                piece = table_ref[index * (wide + 1) + side * reps + rep]
                out_ref[rep, side * rows + index] = piece
        return carry

    lax.fori_loop(0, rows, body, 0, unroll=64)
    nothing = jnp.zeros((lines, lanes), F32)
    for rep in range(reps):
        for side in range(2):
            origin = source_ref[row * wide + side * reps + rep]
            piece = table_ref[lax.div(origin, wide) * (wide + 1) + wide].astype(F32)
            here = lax.rem(origin, wide) == plane
            out_ref[rep, 2 * rows + side] = jnp.where(here, piece, nothing).astype(BF16)
        for slot in range(2 * rows + 2, slots):
            out_ref[rep, slot] = nothing.astype(BF16)


def regroup(place, source, table, reps, slots):
    smem = pl.BlockSpec(memory_space=pltpu.SMEM)
    vmem = pl.BlockSpec(memory_space=pltpu.VMEM)
    return pl.pallas_call(
        regroup_kernel,
        out_shape=jax.ShapeDtypeStruct((reps, slots) + table.shape[1:], table.dtype),
        in_specs=[smem, smem, vmem],
        out_specs=vmem,
        compiler_params=pltpu.CompilerParams(vmem_limit_bytes=8 * 2**20),
        name="regroup",
    )(place, source, table)


def unfold(packed, diagonal, stat_ref):
    half = packed.shape[0]
    folded = packed[:, :half].astype(F32)
    cross = packed[:, half:].astype(F32)
    row, col = grid_of((half, half))
    turned = folded.T
    stat_ref[:half, :half] += jnp.where(row <= col, folded, turned)
    lower = jnp.where(row > col, folded, turned)
    stat_ref[half:, half:] += jnp.where(row == col, diagonal, lower)
    stat_ref[:half, half:] += cross
    stat_ref[half:, :half] += cross.T


def main_kernel(place_ref, packed_ref, pieces_ref, out_ref, grad_ref, left_ref, right_ref):
    core, zl = place_ref[0], place_ref[1]
    cores, steps, rows, size = pieces_ref.shape
    for step in range(steps):
        origin = lax.rem(zl - step + steps, steps)
        for member in range(cores):
            first = pl.multiple_of((origin * cores + member) * rows, rows)
            grad_ref[pl.ds(first, rows), :] = pieces_ref[member, step]
    gradient = grad_ref[...]
    left_ref[...] = matmul(gradient, gradient, ((1,), (1,)))
    right_ref[...] = matmul(gradient.T, gradient)
    planes = [(member, rep) for member in range(cores) for rep in range(packed_ref.shape[1])]
    part = size // 2 // len(planes)
    diagonals = sum(packed_ref[m, r].astype(F32)[2 * part :, : size // 4] for m, r in planes)
    for side, ref in enumerate((left_ref, right_ref)):
        packed = [packed_ref[m, r, side * part : (side + 1) * part, :] for m, r in planes]
        lines = [diagonals[2 * side + line : 2 * side + line + 1, :] for line in range(2)]
        unfold(jnp.concatenate(packed, axis=0), jnp.concatenate(lines, axis=1), ref)
    row, col = grid_of((size, size))
    identity = jnp.where(row == col, 1.0, 0.0)
    images = [jnp.sum(ref[...], axis=0, keepdims=True) for ref in (left_ref, right_ref)]
    for power_step in range(POWER_STEPS):
        axis = 1 - power_step % 2
        scales = [lax.rsqrt(jnp.sum(image * image) + EPSILON) for image in images]
        vectors = images
        images = [
            jnp.sum(ref[...] * vector, axis=axis, keepdims=True) * scale
            for ref, vector, scale in zip((left_ref, right_ref), vectors, scales)
        ]
    vectors = [vector * scale for vector, scale in zip(vectors, scales)]
    scaleds = []
    for ref, vector, image in zip((left_ref, right_ref), vectors, images):
        turned = jnp.sum(identity * vector, axis=0, keepdims=True)
        scaleds.append(ref[...] * (1.0 / jnp.sum(turned * image)))
    narrows = [scaled.astype(BF16) for scaled in scaleds]
    times = [1.25 * scaled - 0.25 * matmul(n, n) for scaled, n in zip(scaleds, narrows)]
    squares = [
        (1.5625 * identity - 0.3125 * scaled - 0.25 * t).astype(BF16)
        for scaled, t in zip(scaleds, times)
    ]
    fourths = [matmul(square, square).astype(BF16) for square in squares]
    lasts = [matmul(fourth, t.astype(BF16)) for fourth, t in zip(fourths, times)]
    roots = [
        1.5625 * identity - 0.3125 * scaled - 0.25 * last for scaled, last in zip(scaleds, lasts)
    ]
    left, right = roots
    half_way = matmul(left.astype(BF16), gradient)
    raw = matmul(half_way.astype(BF16), right.astype(BF16))
    wide = gradient.astype(F32)
    scale = jnp.sqrt(jnp.sum(wide * wide) + EPSILON) * lax.rsqrt(
        jnp.sum(raw * raw) + EPSILON
    )
    left_ref[...] = raw
    for origin in range(steps):
        first = pl.multiple_of(origin * cores * rows + core * rows, rows)
        out_ref[origin] = (left_ref[pl.ds(first, rows), :] * scale).astype(BF16)


def precondition(place, packed, pieces):
    size = pieces.shape[-1]
    vmem = pl.BlockSpec(memory_space=pltpu.VMEM)
    return pl.pallas_call(
        main_kernel,
        out_shape=jax.ShapeDtypeStruct(pieces.shape[1:], BF16),
        in_specs=[pl.BlockSpec(memory_space=pltpu.SMEM), vmem, vmem],
        out_specs=vmem,
        scratch_shapes=[
            pltpu.VMEM((size, size), BF16),
            pltpu.VMEM((size, size), F32),
            pltpu.VMEM((size, size), F32),
        ],
        compiler_params=pltpu.CompilerParams(vmem_limit_bytes=40 * 2**20),
        name="precondition",
    )(place, packed, pieces)


def on_device(partials, factor_stats, owner_slots):
    rows, width = partials.shape[1:]
    size = factor_stats.shape[-1]
    reps, zls, cores = (lax.axis_size(name) for name in ("rep", "zl", "core"))
    core, zl, rep = (lax.axis_index(name) for name in ("core", "zl", "rep"))
    plane = cores * reps
    place = jnp.stack([core, zl, rep, lax.axis_index(CHIP_ROWS)]).astype(jnp.int32)

    source = 2 * owner_slots.reshape(-1, 1, reps) + jnp.arange(2, dtype=jnp.int32)[None, :, None]
    source = source.reshape(-1)
    everyone = source.shape[0]

    parts = list(part_columns(place, partials, reps, zls, size))
    for step in range(1, reps):
        route = [(index, (index + step) % reps) for index in range(reps)]
        parts[step] = lax.ppermute(parts[step], "rep", route)

    packed, diagonal = pack_statistic(factor_stats[0, 0])
    tiles = packed.reshape(size // 16, 4, 2, size // 128, 128).transpose(0, 3, 1, 2, 4)
    spread = lax.all_to_all(
        tiles.reshape(everyone, 2, 128), ACROSS, split_axis=0, concat_axis=0, tiled=True
    )
    spread, parts[1], parts[3] = lax.optimization_barrier((spread, parts[1], parts[3]))
    arrival = source % plane * (everyone // plane) + source // plane
    outgoing = select_rows(arrival, spread, diagonal, plane)
    in_row = lax.all_to_all(outgoing, CHIP_ROWS, split_axis=0, concat_axis=0, tiled=True)

    summed = sum(part.astype(F32) for part in parts).astype(BF16)
    pieces = [summed[0]]
    for step in range(1, zls):
        route = [(index, (index + step) % zls) for index in range(zls)]
        pieces.append(lax.ppermute(summed[step], "zl", route))
    in_row, pieces[1] = lax.optimization_barrier((in_row, pieces[1]))
    pieces = lax.all_gather(jnp.stack(pieces), "core")

    slots = 2 * everyone // plane + 16
    outgoing = regroup(place, source, in_row, reps, slots)
    delivered = lax.all_to_all(outgoing, "rep", split_axis=0, concat_axis=0, tiled=True)
    delivered = delivered.reshape(reps, slots // 16, size // 128, 4, 2, 128)
    delivered = delivered.transpose(0, 1, 3, 4, 2, 5).reshape(reps, slots // 2, size)
    delivered = lax.all_gather(delivered, "core")
    update = precondition(place, delivered, pieces)

    update = update.reshape(zls * reps, rows // reps, size)
    arrived = lax.all_to_all(update, ("zl", "rep"), split_axis=0, concat_axis=0, tiled=True)
    return arrived.transpose(1, 0, 2).reshape(rows // reps, width)


def solution(mesh):
    fsdp, reps = mesh.devices.shape
    fine = Mesh(mesh.devices.reshape(4, 4, fsdp // 32, 2, reps), EVERYONE)
    return jax.shard_map(
        on_device,
        mesh=fine,
        in_specs=(P("rep", PLANE, None), P(PLANE, "rep", None, None), P()),
        out_specs=P(EVERYONE, None),
        check_vma=False,
    )
```
